256 devices in a mesh: seq: 8 (over y, core), expert: 16 (over x_hi, z), rep: 2 (over x_lo).
Axes of the slice: x: 4 (x_hi: 2, x_lo: 2; x = x_hi * 2 + x_lo), y: 4, z: 8, core: 2. Of those that a mesh axis runs over, the one named last changes fastest.
Arguments:
- tokens: bfloat16 [2, 1024, 4096], P(None, ('seq', 'expert', 'rep')), may hold values from -6 to 6
- grad_out: bfloat16 [2, 1024, 4096], P(None, ('seq', 'expert', 'rep')), may hold values from -6 to 6
- expert_ids: int32 [2, 1024, 8], P(None, ('seq', 'expert', 'rep')), may hold values from 0 to 15, all different within a row; in each aligned block of 4 rows (0 to 3, 4 to 7, ..., all dimensions but the last counted through in order) at most 3 rows name the same one
- gate_weights: bfloat16 [2, 1024, 8], P(None, ('seq', 'expert', 'rep')), may hold values from 0.25 to 1
- w_gate: bfloat16 [16, 1536, 4096], P('expert', 'seq'), may hold values from -0.09375 to 0.09375
- w_up: bfloat16 [16, 1536, 4096], P('expert', 'seq'), may hold values from -0.09375 to 0.09375
- w_down: bfloat16 [16, 1536, 4096], P('expert', 'seq'), may hold values from -0.15625 to 0.15625
Outputs:
- d_tokens: bfloat16 [2, 1024, 4096], P(None, ('seq', 'expert', 'rep'))
- grad_gate: bfloat16 [16, 1536, 4096], P('expert', 'seq')
- grad_up: bfloat16 [16, 1536, 4096], P('expert', 'seq')
- grad_down: bfloat16 [16, 1536, 4096], P('expert', 'seq')
The draws below stay inside these ranges and needn't reach their ends.
Inputs may be any that keep to these rules, and one draw needn't show every extreme that they name: `expert_ids`: in each aligned block of 4 rows (the rows of one device in one micro-batch) a row names 8 different experts, and no expert is named by more than 3 rows of the block; some expert is named by exactly 3 rows in some blocks.
All inputs are finite; a program needn't handle non-finite values.
Results may differ from the reference program's by a relative error of at most 0.019.
Values may be sent and summed in bfloat16 or wider, within the bound.
A program may use at most 128 MiB of HBM per device.

```python
import math
import jax
import jax.numpy as jnp
import numpy as np
from jax import lax

D = 4096
FF = 1536
TOK_MB = 4
MICRO = 2
EXPERTS = 16
TOP = 8
MOST = 3
TOKENS = 1024
N_SEQ = 8
N_REP = 2


def level_of(rng, shape, cuts, low, high):
    def one(position, blocks):
        heights = jax.random.uniform(jax.random.fold_in(jax.random.fold_in(rng, 6), position), (blocks,), jnp.float32, low / len(cuts), high / len(cuts))
        return jnp.repeat(jnp.exp(heights), shape[position] // blocks).reshape((-1,) + (1,) * (len(shape) - position - 1))

    level = one(*cuts[0])
    for cut in cuts[1:]:
        level = level * one(*cut)
    return level


def assign_block(own_key, own, number, rows, amount, top, reach, slope):
    sequence = jax.random.permutation(own_key, amount)
    heavy_load, ordinary = shares(amount, rows * top, reach, slope, True), shares(amount, rows * top, reach, slope, False)
    places = jnp.arange(amount)

    def named(sizes, offset_by):
        used = int((sizes > 0).sum())
        fixed = max(1, used // 4)
        shifted = fixed + (places - fixed + offset_by * (used - fixed)) % max(1, amount - fixed)
        return jnp.zeros((amount,), jnp.int32).at[sequence[jnp.where(places < fixed, places, shifted)]].set(jnp.asarray(sizes, jnp.int32))

    sizes = jnp.where(number % 4 == 0, named(heavy_load, number // 4), named(ordinary, number - number // 4 - 1))
    mixed = jax.random.permutation(jax.random.fold_in(own, 3), amount)
    giver, receiver = mixed[0:amount // 2 * 2:2], mixed[1:amount // 2 * 2:2]
    slack = jnp.minimum(sizes[giver] - 1, reach - sizes[receiver]) // 2
    slack = jnp.where((giver == sequence[0]) | (receiver == sequence[0]) | (sizes[receiver] == 0), 0, jnp.maximum(slack, 0))
    shifted = jax.random.randint(jax.random.fold_in(own, 4), (amount // 2,), 0, 1 << 20) % (slack + 1)
    sizes = sizes.at[giver].add(-shifted).at[receiver].add(shifted)
    members = jnp.searchsorted(jnp.cumsum(sizes), jnp.arange(rows * top), side="right").astype(jnp.int32)
    table = members.reshape(top, rows).T
    table = table[jax.random.permutation(jax.random.fold_in(own, 1), rows)]
    offset_by = jax.random.randint(jax.random.fold_in(own, 2), (rows, 1), 0, top)
    return jnp.take_along_axis(table, (jnp.arange(top)[None, :] + offset_by) % top, axis=1)


def shares(amount, total, reach, skew, full):
    weights = [(1 << 20) // math.isqrt(grade ** skew) + 1 for grade in range(1, amount + 1)]
    largest = reach if full else min(reach, max(-(-total // amount), total * weights[0] // sum(weights)))
    least = 1 if total - largest >= amount - 1 else 0
    given, spare = [largest] + [least] * (amount - 1), total - largest - least * (amount - 1)
    while spare > 0:
        free = [i for i in range(1, amount) if given[i] < largest] or [i for i in range(1, amount) if given[i] < reach]
        pool, left = sum([weights[i] for i in free]), spare
        for i in free:
            addition = min(reach - given[i], max(1, left * weights[i] // pool), spare)
            given[i] = given[i] + addition
            spare = spare - addition
    return np.array(given)


def gaussian(own_key, dims, deviation, reach, cuts=(), kind=jnp.bfloat16):
    values = deviation * jax.random.normal(own_key, dims, jnp.float32)
    if cuts:
        values = values * level_of(own_key, dims, cuts, -0.22, 0.18)
    return jnp.clip(values, -reach, reach).astype(kind)


def setup_inputs(seed: int = 0) -> dict:
    streams_of = jax.random.split(jax.random.key(seed), 8)
    tokens = gaussian(streams_of[0], (MICRO, TOKENS, D), 1.0, 6.0, ((1, 256),))
    grad_out = gaussian(streams_of[1], (MICRO, TOKENS, D), 0.5, 6.0, ((1, 256),))
    expert_ids_keys = jax.random.split(jax.random.fold_in(streams_of[2], 1), MICRO * TOKENS // TOK_MB)
    expert_ids_turns = jax.random.permutation(jax.random.fold_in(streams_of[2], 3), MICRO * TOKENS // TOK_MB)
    expert_ids = jax.vmap(lambda own, number: assign_block(jax.random.fold_in(streams_of[2], 2), own, number, TOK_MB, EXPERTS, TOP, MOST, 2))(expert_ids_keys, expert_ids_turns).reshape((MICRO, TOKENS, TOP))
    gate_weights = jnp.clip(0.25 + 0.75 * jax.random.uniform(streams_of[3], (MICRO, TOKENS, TOP), jnp.float32) ** level_of(streams_of[3], (MICRO, TOKENS, TOP), ((1, 256),), -0.2, 0.2), 0.25, 1.0).astype(jnp.bfloat16)
    w_gate = gaussian(streams_of[4], (EXPERTS, FF, D), D ** -0.5, 0.09375, ((0, 16), (1, 8)))
    w_up = gaussian(streams_of[5], (EXPERTS, FF, D), D ** -0.5, 0.09375, ((0, 16), (1, 8)))
    w_down = gaussian(streams_of[6], (EXPERTS, FF, D), FF ** -0.5, 0.15625, ((0, 16), (1, 8)))
    return dict(tokens=tokens, grad_out=grad_out, expert_ids=expert_ids, gate_weights=gate_weights, w_gate=w_gate, w_up=w_up, w_down=w_down)


def regroup(array, micro_count, blocks):
    tail = array.shape[2:]
    shaped = array.reshape((micro_count, blocks // N_REP, N_REP, TOK_MB) + tail)
    moved = jnp.moveaxis(shaped, 2, 0)
    return moved.reshape((N_REP * micro_count * (blocks // N_REP) * TOK_MB,) + tail)


def rounded(value):
    return lax.optimization_barrier(value.astype(jnp.bfloat16)).astype(jnp.float32)


def reference(tokens, grad_out, expert_ids, gate_weights, w_gate, w_up, w_down):
    micro_count, total_tokens, top_count = expert_ids.shape
    width = tokens.shape[2]
    hidden_units = w_gate.shape[1]
    slice_units = hidden_units // N_SEQ
    blocks = total_tokens // TOK_MB
    x_all = regroup(tokens, micro_count, blocks)
    dy_all = regroup(grad_out, micro_count, blocks).astype(jnp.float32)
    ids_all = regroup(expert_ids, micro_count, blocks)
    gates_all = regroup(gate_weights, micro_count, blocks).astype(jnp.float32)
    row_count = x_all.shape[0]
    group_rows = row_count // N_REP

    def per_expert(carry, expert):
        coeff = jnp.sum(jnp.where(ids_all == expert, gates_all, 0.0), axis=1)
        scaled = (coeff[:, None] * dy_all).astype(jnp.bfloat16)
        gate_w = lax.dynamic_index_in_dim(w_gate, expert, 0, keepdims=False)
        up_w = lax.dynamic_index_in_dim(w_up, expert, 0, keepdims=False)
        down_w = lax.dynamic_index_in_dim(w_down, expert, 0, keepdims=False)
        gate_pre = jnp.dot(x_all, gate_w.T, preferred_element_type=jnp.float32)
        up_pre = jnp.dot(x_all, up_w.T, preferred_element_type=jnp.float32)
        sigma = jax.nn.sigmoid(gate_pre)
        active = gate_pre * sigma
        hidden = (active * up_pre).astype(jnp.bfloat16)
        d_hidden = jnp.dot(scaled, down_w.T, preferred_element_type=jnp.float32)
        d_up = (d_hidden * active).astype(jnp.bfloat16)
        d_gate = (d_hidden * up_pre * sigma * (1.0 + gate_pre * (1.0 - sigma))).astype(jnp.bfloat16)
        d_rows = carry
        for part in range(N_SEQ):
            low = part * slice_units
            high = low + slice_units
            piece = jnp.dot(d_gate[:, low:high], gate_w[low:high], preferred_element_type=jnp.float32)
            piece = piece + jnp.dot(d_up[:, low:high], up_w[low:high], preferred_element_type=jnp.float32)
            d_rows = d_rows + rounded(piece)
        sum_gate = jnp.zeros((hidden_units, width), jnp.float32)
        sum_up = jnp.zeros((hidden_units, width), jnp.float32)
        sum_down = jnp.zeros((hidden_units, width), jnp.float32)
        for group in range(N_REP):
            low = group * group_rows
            high = low + group_rows
            sum_gate = sum_gate + rounded(jnp.dot(d_gate[low:high].T, x_all[low:high], preferred_element_type=jnp.float32))
            sum_up = sum_up + rounded(jnp.dot(d_up[low:high].T, x_all[low:high], preferred_element_type=jnp.float32))
            sum_down = sum_down + rounded(jnp.dot(hidden[low:high].T, scaled[low:high], preferred_element_type=jnp.float32))
        grads = (sum_gate.astype(jnp.bfloat16), sum_up.astype(jnp.bfloat16), sum_down.astype(jnp.bfloat16))
        return d_rows, grads

    experts = w_gate.shape[0]
    start = jnp.zeros((row_count, width), jnp.float32)
    d_rows, grads = lax.scan(per_expert, start, jnp.arange(experts, dtype=jnp.int32))
    shaped = d_rows.reshape((N_REP, micro_count, blocks // N_REP, TOK_MB, width))
    d_tokens = jnp.moveaxis(shaped, 0, 2).reshape((micro_count, total_tokens, width))
    return d_tokens.astype(jnp.bfloat16), grads[0], grads[1], grads[2]
```

```python
import functools
import heapq

import jax
import jax.numpy as jnp
from jax import lax
from jax.experimental import pallas as pl
from jax.experimental.pallas import tpu as pltpu
from jax.sharding import PartitionSpec as P

MESH = pl.DeviceIdType.MESH
LANES = 128
ALL = ("seq", "expert", "rep")

ORDERS = ((0, 1, 2), (1, 2, 0), (2, 0, 1))


def gather_events(dims, unit):
    link, ready, arrived, count = {}, [], [], 0
    left = {}

    def steps(n, phase, direction):
        if n == 2:
            return 1 if direction == 1 else 0
        half = n // 2
        return half if phase > 0 or direction == 1 else half - 1

    def size(stream, phase, step):
        order = ORDERS[stream]
        blocks = 1
        for axis in order[:phase]:
            blocks *= dims[axis]
        n = dims[order[phase]]
        return blocks / 2 if (phase > 0 and n > 2 and step == n // 2) else blocks

    def begin(now, stream, phase):
        nonlocal count
        n = dims[ORDERS[stream][phase]]
        left[stream, phase] = sum(steps(n, phase, d) for d in (1, -1))
        for d in (1, -1):
            if steps(n, phase, d):
                heapq.heappush(ready, (now, count, stream, phase, d, 1))
                count += 1

    for stream in range(3):
        begin(0.0, stream, 0)
    pending = []
    while ready or pending:
        if ready and (not pending or ready[0][0] <= pending[0][0]):
            now, _, stream, phase, d, step = heapq.heappop(ready)
            axis = ORDERS[stream][phase]
            start = max(now, link.get((axis, d), 0.0))
            end = start + size(stream, phase, step) * unit
            link[axis, d] = end
            heapq.heappush(pending, (end + 1.0, count, stream, phase, d, step))
            count += 1
        else:
            now, _, stream, phase, d, step = heapq.heappop(pending)
            arrived.append((stream, phase, d, step))
            n = dims[ORDERS[stream][phase]]
            if step < steps(n, phase, d):
                heapq.heappush(ready, (now, count, stream, phase, d, step + 1))
                count += 1
            left[stream, phase] -= 1
            if left[stream, phase] == 0 and phase < 2:
                begin(now, stream, phase + 1)
    return arrived, steps, link


def gather_kernel(dims, l_ref, g_ref, got, both, send, recv, sib_send, sib_recv, pair_send, pair_recv, local):
    columns = l_ref.shape[1] // 3
    seq, expert, rep = lax.axis_index("seq"), lax.axis_index("expert"), lax.axis_index("rep")
    core = lax.rem(seq, 2)
    place = (2 * (expert // dims[2]) + rep, seq // 2, lax.rem(expert, dims[2]))

    def device(at, which):
        x, y, z = at
        return {"seq": 2 * y + which, "expert": (x // 2) * dims[2] + z, "rep": lax.rem(x, 2)}

    def neighbour(axis, d):
        at = list(place)
        at[axis] = lax.rem(at[axis] + d + dims[axis], dims[axis])
        return device(at, core)

    sibling = device(place, 1 - core)
    near = [sibling] + [neighbour(axis, d) for axis in range(3) for d in ((1, -1) if dims[axis] > 2 else (1,))]
    barrier = pltpu.get_barrier_semaphore()
    for other in near:
        pl.semaphore_signal(barrier, inc=1, device_id=other, device_id_type=MESH)
    pl.semaphore_wait(barrier, len(near))

    pair = pltpu.make_async_remote_copy(
        src_ref=l_ref, dst_ref=got, send_sem=pair_send, recv_sem=pair_recv, device_id=sibling, device_id_type=MESH)
    pair.start()
    pair.wait()
    mine, other = l_ref[...].astype(jnp.float32), got[...].astype(jnp.float32)
    first = jnp.where(core == 0, mine, other)
    second = jnp.where(core == 0, other, mine)
    half = l_ref.shape[0] // 2
    both[0] = jnp.concatenate([first[:half], second[:half]], axis=0).astype(jnp.bfloat16)
    both[1] = jnp.concatenate([first[half:], second[half:]], axis=0).astype(jnp.bfloat16)
    x, y, z = place
    own = pltpu.make_async_copy(both, g_ref.at[:, x, y, z], local)
    own.start()
    own.wait()

    def chunk(which, stream, phase, index, part):
        order = ORDERS[stream]
        at = [None] * 3
        for position, axis in enumerate(order):
            if position < phase:
                at[axis] = slice(None)
            elif position == phase:
                at[axis] = index
            else:
                at[axis] = place[axis]
        if part is not None:
            n = dims[order[0]]
            at[order[0]] = pl.ds(part * (n // 2), n // 2)
        return g_ref.at[which, at[0], at[1], at[2], :, pl.ds(stream * columns, columns)]

    arrived, steps, _ = gather_events(dims, 0.9)
    number = {event: i for i, event in enumerate(arrived)}

    def part_of(event):
        stream, phase, d, step = event
        n = dims[ORDERS[stream][phase]]
        if phase == 0 or n == 2 or step < n // 2:
            return None
        return 0 if d == 1 else 1

    def ring(event, incoming):
        stream, phase, d, step = event
        axis = ORDERS[stream][phase]
        n = dims[axis]
        index = lax.rem(place[axis] - d * (step if incoming else step - 1) + n, n)
        ref = chunk(core, stream, phase, index, part_of(event))
        i = number[event]
        return pltpu.make_async_remote_copy(
            src_ref=ref, dst_ref=ref, send_sem=send.at[i], recv_sem=recv.at[i],
            device_id=neighbour(axis, d), device_id_type=MESH)

    def across(event, incoming):
        stream, phase, d, step = event
        axis = ORDERS[stream][phase]
        n = dims[axis]
        index = lax.rem(place[axis] - d * step + n, n)
        ref = chunk(1 - core if incoming else core, stream, phase, index, part_of(event))
        i = number[event]
        return pltpu.make_async_remote_copy(
            src_ref=ref, dst_ref=ref, send_sem=sib_send.at[i], recv_sem=sib_recv.at[i],
            device_id=sibling, device_id_type=MESH)

    left = {}

    def begin(stream, phase):
        n = dims[ORDERS[stream][phase]]
        left[stream, phase] = 0
        for d in (1, -1):
            left[stream, phase] += steps(n, phase, d)
            if steps(n, phase, d):
                ring((stream, phase, d, 1), False).start()

    for stream in range(3):
        begin(stream, 0)
    for event in arrived:
        stream, phase, d, step = event
        ring(event, True).wait_recv()
        n = dims[ORDERS[stream][phase]]
        if step < steps(n, phase, d):
            ring((stream, phase, d, step + 1), False).start()
        left[stream, phase] -= 1
        if left[stream, phase] == 0 and phase < 2:
            begin(stream, phase + 1)
        across(event, False).start()
    for event in arrived:
        across(event, True).wait_recv()
    for event in arrived:
        ring(event, False).wait_send()
        across(event, False).wait_send()


def gather(dims, block):
    columns = block.shape[1]
    count = len(gather_events(dims, 0.9)[0])
    sems = lambda n: pltpu.SemaphoreType.DMA((n,))
    return pl.pallas_call(
        functools.partial(gather_kernel, dims),
        out_shape=jax.ShapeDtypeStruct((2,) + dims + (block.shape[0], columns), jnp.bfloat16),
        in_specs=[pl.BlockSpec(memory_space=pltpu.VMEM)],
        out_specs=pl.BlockSpec(memory_space=pl.ANY),
        scratch_shapes=[
            pltpu.VMEM(block.shape, jnp.bfloat16),
            pltpu.VMEM((2,) + block.shape, jnp.bfloat16),
            sems(count), sems(count), sems(count), sems(count),
            pltpu.SemaphoreType.DMA, pltpu.SemaphoreType.DMA, pltpu.SemaphoreType.DMA,
        ],
        compiler_params=pltpu.CompilerParams(collective_id=0, has_side_effects=True),
    )(block)


def dot(a, b, dims):
    return lax.dot_general(a, b, (dims, ((), ())), preferred_element_type=jnp.float32)


def forward_kernel(width, x_ref, dy_ref, wg_ref, wu_ref, wd_ref, d_ref, t_ref):
    rows = d_ref.shape[0]
    units = wg_ref.shape[0]
    x = x_ref[...].reshape(rows, x_ref.shape[-1])
    dy = dy_ref[...].reshape(rows, x_ref.shape[-1])[:, :width]
    coeff = x[:, width:].astype(jnp.float32)
    x = x[:, :width]
    lane = lax.broadcasted_iota(jnp.int32, coeff.shape, 1)
    c = jnp.sum(jnp.where(lane == lax.axis_index("expert"), coeff, 0.0), axis=1, keepdims=True)
    gate_pre = dot(x, wg_ref[...], ((1,), (1,)))
    up_pre = dot(x, wu_ref[...], ((1,), (1,)))
    d_hidden = c * dot(dy, wd_ref[...], ((1,), (1,)))
    sigma = 1.0 / (1.0 + jnp.exp(-gate_pre))
    active = gate_pre * sigma
    hidden = c * (active * up_pre)
    d_up = d_hidden * active
    d_gate = d_hidden * up_pre * sigma * (1.0 + gate_pre * (1.0 - sigma))
    d_ref[:, :units] = d_gate.astype(jnp.bfloat16)
    d_ref[:, units:] = d_up.astype(jnp.bfloat16)
    for i, value in enumerate((d_gate, d_up, hidden)):
        t_ref[i] = value.T.astype(jnp.bfloat16)


def forward(dims, gathered, wg, wu, wd):
    units, width = wg.shape
    x, y, z = dims
    rows = 2 * z * 16
    total = x * y * z * 16
    columns = gathered.shape[-1]
    block = lambda which: pl.BlockSpec((None, None, 2, z, 16, columns), lambda i: (which, i // (y // 2), i % (y // 2), 0, 0, 0))
    whole = pl.BlockSpec((units, width), lambda i: (0, 0), pipeline_mode=pl.Buffered(1))
    return pl.pallas_call(
        functools.partial(forward_kernel, width),
        grid=(x * y // 2,),
        out_shape=(jax.ShapeDtypeStruct((total, 2 * units), jnp.bfloat16), jax.ShapeDtypeStruct((3, units, total), jnp.bfloat16)),
        in_specs=[block(0), block(1), whole, whole, whole],
        out_specs=(pl.BlockSpec((rows, 2 * units), lambda i: (i, 0)), pl.BlockSpec((3, units, rows), lambda i: (0, 0, i))),
        compiler_params=pltpu.CompilerParams(vmem_limit_bytes=48 << 20),
    )(gathered, gathered, wg, wu, wd)


def weight_kernel(t_ref, x_ref, dy_ref, gate_ref, up_ref, down_ref):
    units, rows = t_ref.shape[1:]
    x = x_ref[...].reshape(rows, x_ref.shape[-1])
    dy = dy_ref[...].reshape(rows, x_ref.shape[-1])
    gate_ref[...] = dot(t_ref[0], x, ((1,), (0,))).astype(jnp.bfloat16)
    up_ref[...] = dot(t_ref[1], x, ((1,), (0,))).astype(jnp.bfloat16)
    down_ref[...] = dot(t_ref[2], dy, ((1,), (0,))).astype(jnp.bfloat16)


def weight_grads(dims, width, turned, gathered):
    units = turned.shape[1]
    tile = min(512, width)
    block = lambda which: pl.BlockSpec((None,) + dims + (16, tile), lambda i: (which, 0, 0, 0, 0, i))
    out = pl.BlockSpec((units, tile), lambda i: (0, i))
    return pl.pallas_call(
        weight_kernel,
        grid=(width // tile,),
        out_shape=[jax.ShapeDtypeStruct((units, width), jnp.bfloat16)] * 3,
        in_specs=[pl.BlockSpec(turned.shape, lambda i: (0, 0, 0), pipeline_mode=pl.Buffered(1)), block(0), block(1)],
        out_specs=[out] * 3,
        compiler_params=pltpu.CompilerParams(vmem_limit_bytes=48 << 20),
    )(turned, gathered, gathered)


AXES = ((2, 1), (1, 2))


def scatter_steps(dims, stream, phase, d):
    if phase == 2:
        return 1 if d == 1 else 0
    return dims[AXES[stream][phase]] // 2


def scatter_events(dims, shares, unit):
    link, ready, arrived, left = {}, [], [], {}
    count = 0

    def size(stream, phase, step):
        if phase == 2:
            return shares[stream]
        blocks = 2 * (dims[AXES[stream][1]] if phase == 0 else 1)
        return shares[stream] * blocks / (2 if step == dims[AXES[stream][phase]] // 2 else 1)

    def begin(now, stream, phase):
        nonlocal count
        left[stream, phase] = sum(1 for d in (1, -1) if scatter_steps(dims, stream, phase, d))
        for d in (1, -1):
            if scatter_steps(dims, stream, phase, d):
                heapq.heappush(ready, (now, count, stream, phase, d, scatter_steps(dims, stream, phase, d)))
                count += 1

    for stream in (0, 1):
        begin(0.0, stream, 0)
    pending = []
    while ready or pending:
        if ready and (not pending or ready[0][0] <= pending[0][0]):
            now, _, stream, phase, d, step = heapq.heappop(ready)
            axis = AXES[stream][phase] if phase < 2 else 0
            end = max(now, link.get((axis, d), 0.0)) + size(stream, phase, step) * unit
            link[axis, d] = end
            heapq.heappush(pending, (end + 2.0, count, stream, phase, d, step))
            count += 1
        else:
            now, _, stream, phase, d, step = heapq.heappop(pending)
            arrived.append((stream, phase, d, step))
            if step > 1:
                heapq.heappush(ready, (now, count, stream, phase, d, step - 1))
                count += 1
            else:
                left[stream, phase] -= 1
                if left[stream, phase] == 0 and phase < 2:
                    begin(now, stream, phase + 1)
    return arrived


def scatter_kernel(dims, shares, arrived, d_ref, wg_ref, wu_ref, out_ref, own, away, near, *rest):
    count = len(arrived)
    lands, last, (send, recv, pass_send, pass_recv, end_send, end_recv) = rest[:count], rest[count], rest[count + 1:]
    units = wg_ref.shape[0]
    half = wg_ref.shape[1] // 2
    seq, expert, rep = lax.axis_index("seq"), lax.axis_index("expert"), lax.axis_index("rep")
    core = lax.rem(seq, 2)
    place = (expert // dims[2], seq // 2, lax.rem(expert, dims[2]))
    sizes = (2, dims[1], dims[2])

    def device(at, which):
        return {"seq": 2 * at[1] + which, "expert": at[0] * dims[2] + at[2], "rep": rep}

    def neighbour(axis, d):
        at = list(place)
        at[axis] = lax.rem(at[axis] + d + sizes[axis], sizes[axis])
        return device(at, core)

    sibling = device(place, 1 - core)
    around = [sibling, neighbour(0, 1)] + [neighbour(axis, d) for axis in (1, 2) for d in (1, -1)]
    barrier = pltpu.get_barrier_semaphore()
    for other in around:
        pl.semaphore_signal(barrier, inc=1, device_id=other, device_id_type=MESH)
    pl.semaphore_wait(barrier, len(around))

    starts = (0, shares[0] * LANES)
    lanes = lambda stream: pl.ds(starts[stream], shares[stream] * LANES)
    pieces = []
    for stream in (0, 1):
        n = dims[AXES[stream][0]]
        offsets = [n // 2] + [d * k for k in range(n // 2 - 1, 0, -1) for d in (1, -1)] + [0]
        pieces += [((i + 0.5) / n, stream, offset) for i, offset in enumerate(offsets)]
    pieces = [piece[1:] for piece in sorted(pieces)]
    number = {piece: i for i, piece in enumerate(pieces)}

    def offset_index(axis, offset):
        return lax.rem(place[axis] + offset + sizes[axis], sizes[axis])

    def index(stream, offset):
        i = offset_index(AXES[stream][0], offset)
        return (slice(None), slice(None), i) if stream == 0 else (slice(None), i)

    def product(stream, offset, side, target):
        rows = d_ref[(slice(None), rep) + index(stream, offset)[1:]]
        shape = rows.shape[:-1]
        rows = rows.reshape(-1, 2 * units)
        cols = pl.ds(pl.multiple_of(side * half + starts[stream], LANES), shares[stream] * LANES)
        value = dot(rows[:, :units], wg_ref[:, cols], ((1,), (0,))) + dot(rows[:, units:], wu_ref[:, cols], ((1,), (0,)))
        target[index(stream, offset) + (Ellipsis, lanes(stream))] = value.astype(jnp.bfloat16).reshape(shape + (shares[stream] * LANES,))

    def passing(piece):
        stream, offset = piece
        at = index(stream, offset)
        at = at + (slice(None),) * (4 - len(at)) + (lanes(stream),)
        i = number[piece]
        return pltpu.make_async_remote_copy(
            src_ref=away.at[at], dst_ref=near.at[at], send_sem=pass_send.at[i], recv_sem=pass_recv.at[i],
            device_id=sibling, device_id_type=MESH)

    for piece in pieces:
        product(*piece, 1 - core, away)
        passing(piece).start()
    for piece in pieces:
        product(*piece, core, own)

    summed = set()

    def sum_piece(piece):
        if piece in summed:
            return
        summed.add(piece)
        passing(piece).wait_recv()
        at = index(*piece) + (Ellipsis, lanes(piece[0]))
        own[at] = own[at] + near[at]

    def chunk(event):
        stream, phase, d, step = event
        first, second = AXES[stream]
        at = [slice(None)] * 3
        if phase == 2:
            at = [1 - place[0], place[1], place[2]]
        else:
            at[(first, second)[phase]] = offset_index((first, second)[phase], d * step)
            if phase == 1:
                at[first] = place[first]
            if step == dims[(first, second)[phase]] // 2:
                at[0] = pl.ds(0 if d == 1 else 1, 1)
        return tuple(at)

    order = {event: i for i, event in enumerate(arrived)}

    def ring(event):
        stream, phase, d, step = event
        i = order[event]
        axis = AXES[stream][phase] if phase < 2 else 0
        return pltpu.make_async_remote_copy(
            src_ref=own.at[chunk(event) + (slice(None), lanes(stream))], dst_ref=lands[i], send_sem=send.at[i], recv_sem=recv.at[i],
            device_id=neighbour(axis, d), device_id_type=MESH)

    def begin(stream, phase):
        for d in (1, -1):
            step = scatter_steps(dims, stream, phase, d)
            if step:
                if phase == 0:
                    sum_piece((stream, step))
                ring((stream, phase, d, step)).start()

    left = {(stream, phase): (1 if phase == 2 else 2) for stream in (0, 1) for phase in (0, 1, 2)}
    for stream in (0, 1):
        begin(stream, 0)
    waiting = [piece for piece in pieces if piece not in summed]
    for event in arrived:
        stream, phase, d, step = event
        for _ in range(2):
            if waiting:
                sum_piece(waiting.pop(0))
        if phase == 0:
            sum_piece((stream, d * (step - 1)))
        ring(event).wait_recv()
        i = order[event]
        if phase == 2:
            at = (place[0], place[1], place[2])
        elif step == dims[AXES[stream][phase]] // 2:
            at = list(chunk((stream, phase, d, step - 1)))
            at[0] = pl.ds(0 if d == 1 else 1, 1)
            at = tuple(at)
        else:
            at = chunk((stream, phase, d, step - 1))
        at = at + (Ellipsis, lanes(stream))
        own[at] = own[at] + lands[i][...]
        if step > 1:
            ring((stream, phase, d, step - 1)).start()
        else:
            left[stream, phase] -= 1
            if left[stream, phase] == 0 and phase < 2:
                begin(stream, phase + 1)

    end = pltpu.make_async_remote_copy(
        src_ref=own.at[place[0], place[1], place[2]], dst_ref=last, send_sem=end_send, recv_sem=end_recv,
        device_id=sibling, device_id_type=MESH)
    end.start()
    for piece in pieces:
        passing(piece).wait_send()
    for event in arrived:
        ring(event).wait_send()
    end.wait()
    mine = own[place[0], place[1], place[2]].astype(jnp.float32)
    other = last[...].astype(jnp.float32)
    rows = mine.shape[0] // 2
    left_half = jnp.where(core == 0, mine[:rows], other[rows:])
    right_half = jnp.where(core == 0, other[:rows], mine[rows:])
    out_ref[:, :half] = left_half.astype(jnp.bfloat16)
    out_ref[:, half:] = right_half.astype(jnp.bfloat16)


def scatter(dims, d, wg, wu):
    units, width = wg.shape
    tiles = width // 2 // LANES
    shares = (tiles * 7 // 16, tiles - tiles * 7 // 16)
    arrived = scatter_events(dims, shares, 0.086)
    lands = []
    for stream, phase, way, step in arrived:
        columns = shares[stream] * LANES
        if phase == 2:
            lands.append((16, columns))
            continue
        n = dims[AXES[stream][phase]]
        blocks = (1 if step == n // 2 else 2,)
        lands.append(blocks + ((dims[AXES[stream][1]],) if phase == 0 else ()) + (16, columns))
    half = (2,) + dims[1:] + (16, width // 2)
    sems = lambda n: pltpu.SemaphoreType.DMA((n,))
    vmem = pl.BlockSpec(memory_space=pltpu.VMEM)
    count, pieces = len(arrived), dims[1] + dims[2]
    return pl.pallas_call(
        functools.partial(scatter_kernel, dims, shares, arrived),
        out_shape=jax.ShapeDtypeStruct((8, width), jnp.bfloat16),
        in_specs=[vmem] * 3,
        out_specs=vmem,
        scratch_shapes=[pltpu.VMEM(half, jnp.bfloat16)] * 3
        + [pltpu.VMEM(shape, jnp.bfloat16) for shape in lands]
        + [pltpu.VMEM((16, width // 2), jnp.bfloat16)]
        + [sems(count), sems(count), sems(pieces), sems(pieces), pltpu.SemaphoreType.DMA, pltpu.SemaphoreType.DMA],
        compiler_params=pltpu.CompilerParams(collective_id=1, has_side_effects=True, vmem_limit_bytes=48 << 20),
    )(d.reshape((2, 2) + dims[1:] + (16, 2 * units)), wg, wu)


def body(tokens, grad_out, expert_ids, gate_weights, w_gate, w_up, w_down):
    experts = lax.axis_size("expert")
    dims = (2 * lax.axis_size("rep"), lax.axis_size("seq") // 2, experts // 2)
    micro, rows, _ = expert_ids.shape
    width = tokens.shape[2]
    local = micro * rows
    hits = expert_ids[..., None] == jnp.arange(experts, dtype=jnp.int32)
    coeff = jnp.sum(jnp.where(hits, gate_weights[..., None], 0), axis=2).astype(jnp.bfloat16).reshape(local, experts)
    first = jnp.concatenate([tokens.reshape(local, width), jnp.pad(coeff, ((0, 0), (0, LANES - experts)))], axis=1)
    second = jnp.pad(grad_out.reshape(local, width), ((0, 0), (0, LANES)))
    gathered = gather(dims, jnp.concatenate([first, second], axis=0))
    d, turned = forward(dims, gathered, w_gate[0], w_up[0], w_down[0])
    d_tokens = scatter(dims, d, w_gate[0], w_up[0])
    grads = weight_grads(dims, width, turned, gathered)
    return (d_tokens.reshape(micro, rows, width),) + tuple(g[None] for g in grads)


def solution(mesh):
    rows = P(None, ALL, None)
    weights = P("expert", "seq", None)
    return jax.shard_map(
        body,
        mesh=mesh,
        in_specs=(rows, rows, rows, rows, weights, weights, weights),
        out_specs=(rows, weights, weights, weights),
        check_vma=False,
    )
```

```python
import functools
import heapq
import itertools

import jax
import jax.numpy as jnp
from jax import lax
from jax.experimental import pallas as pl
from jax.experimental.pallas import tpu as pltpu
from jax.sharding import PartitionSpec as P

MESH = pl.DeviceIdType.MESH
LANES = 128
ALL = ("seq", "expert", "rep")

ORDERS = ((0, 1, 2), (2, 1, 0), (2, 0, 1))
BACK = ((0, 1, 2), (0, 2, 1))


def offsets(n):
    return [0] + [d * k for k in range(1, n // 2) for d in (1, -1)] + [n // 2]


def reaches(n, turn):
    return [(d, m) for d, m in ((1, n // 2 - turn % 2), (-1, n // 2 - 1 + turn % 2)) if m]


class Plan:
    def __init__(self, dims, orders, tiles, unit=0.0862, latency=1.75):
        self.dims, self.orders, self.tiles, self.unit, self.latency = dims, orders, tiles, unit, latency
        self.arrived, self.after, self.time = [], {}, {}
        link, ready, pending, got, tick = {}, [], [], {}, itertools.count()

        def begin(now, stream, phase, piece):
            first = [(stream, phase, piece, d, 1) for d, _ in self.ways(stream, phase, piece)]
            for message in first:
                heapq.heappush(ready, (now, next(tick), message))
            return first

        self.first = [m for s in range(len(orders)) for phase in (0, 1) for m in begin(0.0, s, phase, 0)]
        while ready or pending:
            if ready and (not pending or ready[0][0] <= pending[0][0]):
                now, _, message = heapq.heappop(ready)
                heapq.heappush(pending, (self.sent(link, now, message), next(tick), message))
                continue
            now, _, message = heapq.heappop(pending)
            self.arrived.append(message)
            self.time[message] = now
            stream, phase, piece, d, hop = message
            sets_off = []
            if hop < dict(self.ways(stream, phase, piece))[d]:
                sets_off.append((stream, phase, piece, d, hop + 1))
                heapq.heappush(ready, (now, next(tick), sets_off[0]))
            off = self.offset(message)
            got[stream, phase, off] = got.get((stream, phase, off), 0) + 1
            got[stream, phase] = got.get((stream, phase), 0) + 1
            if phase == 0:
                sets_off += begin(now, stream, 1, off)
                if got[stream, 0] == self.ring(stream, 0) - 1:
                    sets_off += begin(now, stream, 2, 0)
            elif phase == 1 and got[stream, 1, off] == self.ring(stream, 0):
                sets_off += begin(now, stream, 2, off)
            self.after[message] = sets_off

    def ring(self, stream, phase):
        return self.dims[self.orders[stream][phase]]

    def ways(self, stream, phase, piece):
        turn = offsets(self.ring(stream, phase - 1)).index(piece) if phase else 0
        return reaches(self.ring(stream, phase), turn)

    def sent(self, link, now, message):
        stream, phase, _, d, _ = message
        key = self.orders[stream][phase], d
        link[key] = max(now, link.get(key, 0.0)) + self.unit * self.tiles[stream] * (self.ring(stream, 0) if phase == 2 else 1)
        return link[key] + self.latency

    def offset(self, message):
        stream, phase, _, d, hop = message
        n = self.ring(stream, phase)
        return n // 2 if 2 * hop == n else -d * hop


class Back(Plan):
    def __init__(self, *args):
        super().__init__(*args)
        messages = list(reversed(self.arrived))
        self.needs = {m: self.needed(m) for m in messages}
        self.first = [m for m in messages if not self.needs[m]]
        link, done, came = {}, set(), []
        ready = [(0.0, i, m) for i, m in enumerate(messages) if not self.needs[m]]
        rank = {m: i for i, m in enumerate(messages)}
        pending, started = [], set(self.first)
        while ready or pending:
            if ready and (not pending or ready[0][0] <= pending[0][0]):
                now, i, message = heapq.heappop(ready)
                heapq.heappush(pending, (self.sent(link, now, message), i, message))
                continue
            now, _, message = heapq.heappop(pending)
            done.add(message)
            came.append(message)
            self.time[message] = now
            self.after[message] = [m for m in messages if m not in started and self.needs[m] <= done]
            for m in self.after[message]:
                started.add(m)
                heapq.heappush(ready, (now, rank[m], m))
        self.arrived = came

    def needed(self, message):
        stream, phase, piece, d, hop = message
        off = self.offset(message)
        needs = set()
        if hop < dict(self.ways(stream, phase, piece))[d]:
            needs.add((stream, phase, piece, d, hop + 1))
        if phase < 2:
            needs |= {(stream, phase + 1, off, way, 1) for way, _ in self.ways(stream, phase + 1, off)}
        if phase == 0:
            needs |= {(stream, 2, 0, way, 1) for way, _ in self.ways(stream, 2, 0)}
        return needs


def dot(a, b, dims):
    return lax.dot_general(a, b, (dims, ((), ())), preferred_element_type=jnp.float32)


def layer_kernel(dims, plan, back, lag,
                 tok_hbm, grad_hbm, ids_hbm, gates_hbm, wg_hbm, wu_hbm, wd_hbm,
                 g_ref, out_ref, gate_hbm, up_hbm, down_hbm,
                 tok_ref, grad_ref, ids_ref, gates_ref, block, got, both, wg_ref, wu_ref, wd_ref, wcat, stage, acc, c_ref,
                 dcat, turned, tiles_ref, grads_ref, own, land, last,
                 in_sem, weight_sem, half_sem, wsend, wrecv, pair_send, pair_recv, local,
                 send, recv, sib_send, sib_recv, load_sem, dsend, drecv, bsend, brecv, tile_sem, grad_sem, end_send, end_recv):
    units, width = wg_ref.shape
    half = width // 2
    micro = tok_ref.shape[0]
    tiles = plan.tiles
    starts = [sum(tiles[:s]) * LANES for s in range(3)]
    seq, expert, rep = lax.axis_index("seq"), lax.axis_index("expert"), lax.axis_index("rep")
    core = lax.rem(seq, 2)
    place = (2 * (expert // dims[2]) + rep, seq // 2, lax.rem(expert, dims[2]))

    def many(pairs, sem):
        return [pltpu.make_async_copy(a, b, sem.at[i]) for i, (a, b) in enumerate(pairs)]

    inputs = many(((tok_hbm, tok_ref), (grad_hbm, grad_ref), (ids_hbm, ids_ref), (gates_hbm, gates_ref)), in_sem)
    weights = many(((wg_hbm, wg_ref), (wu_hbm, wu_ref), (wd_hbm, wd_ref)), weight_sem)
    mine_half = pl.ds(pl.multiple_of(core * half, LANES), half)
    other_half = pl.ds(pl.multiple_of((1 - core) * half, LANES), half)
    halves = many(((wg_hbm.at[:, mine_half], wcat.at[pl.ds(0, units)]), (wu_hbm.at[:, mine_half], wcat.at[pl.ds(units, units)])), half_sem)
    for copy in inputs:
        copy.start()

    def device(at, which):
        x, y, z = at
        return {"seq": 2 * y + which, "expert": (x // 2) * dims[2] + z, "rep": lax.rem(x, 2)}

    def shifted(axis, offset):
        return lax.rem(place[axis] + offset + dims[axis], dims[axis])

    def neighbour(axis, d):
        at = list(place)
        at[axis] = shifted(axis, d)
        return device(at, core)

    sibling = device(place, 1 - core)
    around = [sibling] + [neighbour(axis, d) for axis in range(3) for d in (1, -1)] + [neighbour(0, 2)]
    barrier = pltpu.get_barrier_semaphore()
    for other in around:
        pl.semaphore_signal(barrier, inc=1, device_id=other, device_id_type=MESH)
    for copy in inputs:
        copy.wait()

    rows_of = lambda ref: jnp.concatenate([ref[m].astype(jnp.float32) for m in range(micro)], axis=0)
    ids = jnp.concatenate([ids_ref[m] for m in range(micro)], axis=0)
    gates = rows_of(gates_ref)
    lane = lax.broadcasted_iota(jnp.int32, (ids.shape[0], LANES), 1)
    coeff = jnp.zeros(lane.shape, jnp.float32)
    for k in range(ids.shape[1]):
        coeff = coeff + jnp.where(lane == ids[:, k:k + 1], gates[:, k:k + 1], 0.0)
    block[:, :width] = jnp.concatenate([rows_of(tok_ref), rows_of(grad_ref)], axis=0).astype(jnp.bfloat16)
    block[:, width:] = jnp.concatenate([coeff, jnp.zeros_like(coeff)], axis=0).astype(jnp.bfloat16)
    pl.semaphore_wait(barrier, len(around))

    pair = pltpu.make_async_remote_copy(
        src_ref=block, dst_ref=got, send_sem=pair_send, recv_sem=pair_recv, device_id=sibling, device_id_type=MESH)
    pair.start()
    for copy in weights + halves:
        copy.start()
    pair.wait()
    mine, other = block[...].astype(jnp.float32), got[...].astype(jnp.float32)
    first = jnp.where(core == 0, mine, other)
    second = jnp.where(core == 0, other, mine)
    rows = block.shape[0] // 2
    upper = jnp.concatenate([first[:rows], second[:rows]], axis=0)
    lower = jnp.concatenate([first[rows:], second[rows:]], axis=0)
    both[...] = jnp.where(core == 0, upper, lower).astype(jnp.bfloat16)
    x, y, z = place
    copy = pltpu.make_async_copy(both, g_ref.at[core, x, y, z], local)
    copy.start()
    copy.wait()

    def chunk(which, stream, phase, piece, offset):
        a, b, c = ORDERS[stream]
        at = [None] * 3
        if phase == 0:
            at[a], at[b], at[c] = shifted(a, offset), place[b], place[c]
        elif phase == 1:
            at[a], at[b], at[c] = shifted(a, piece), shifted(b, offset), place[c]
        elif piece is None:
            at[a], at[b], at[c] = slice(None), slice(None), shifted(c, offset)
        else:
            at[a], at[b], at[c] = slice(None), shifted(b, piece), shifted(c, offset)
        return g_ref.at[which, at[0], at[1], at[2], :, pl.ds(starts[stream], tiles[stream] * LANES)]

    number = {message: i for i, message in enumerate(plan.arrived)}

    def ring(message, incoming):
        stream, phase, piece, d, hop = message
        ref = chunk(core, stream, phase, piece, -d * (hop if incoming else hop - 1))
        i = number[message]
        return pltpu.make_async_remote_copy(
            src_ref=ref, dst_ref=ref, send_sem=send.at[i], recv_sem=recv.at[i],
            device_id=neighbour(ORDERS[stream][phase], d), device_id_type=MESH)

    copies = [(s, None, 0) for s in range(3)] + [(m[0], m[2], plan.offset(m)) for m in plan.arrived if m[1] == 2]
    place_of = {copy: i for i, copy in enumerate(copies)}

    def across(copy, incoming):
        stream, piece, offset = copy
        ref = chunk(1 - core if incoming else core, stream, 2, piece, offset)
        i = place_of[copy]
        return pltpu.make_async_remote_copy(
            src_ref=ref, dst_ref=ref, send_sem=sib_send.at[i], recv_sem=sib_recv.at[i],
            device_id=sibling, device_id_type=MESH)

    due = {}
    for message in plan.arrived:
        key = message[0], (plan.offset(message) if message[1] == 2 else 0)
        due[key] = max(due.get(key, 0.0), plan.time[message])
    tasks = sorted(due, key=lambda key: due[key])

    def shape_of(stream):
        return tuple(dims[axis] for axis in sorted(ORDERS[stream][:2]))

    def fetch(task):
        stream, offset = task
        slot = tasks.index(task) % 2
        one, two = shape_of(stream)
        return [pltpu.make_async_copy(
            chunk(which, stream, 2, None, offset),
            stage.at[slot, which, pl.ds(0, one), pl.ds(0, two), :, pl.ds(0, tiles[stream] * LANES)],
            load_sem.at[slot, which]) for which in (0, 1)]

    def load(task):
        stream, offset = task
        for copy in copies:
            if copy[0] == stream and copy[2] == offset:
                across(copy, True).wait_recv()
        for copy in fetch(task):
            copy.start()

    def compute(task):
        stream, offset = task
        slot = tasks.index(task) % 2
        one, two = shape_of(stream)
        for copy in fetch(task):
            copy.wait()
        at = [slice(None)] * 3
        at[ORDERS[stream][2]] = shifted(ORDERS[stream][2], offset)
        columns = tiles[stream] * LANES
        depth = min(columns, width - starts[stream])
        part = pl.ds(starts[stream], depth)
        step = min(one, max(1, 256 // (two * 16)))

        @pl.loop(0, one // step)
        def _(i):
            some = pl.ds(i * step, step)
            x, dy = (stage[slot, which, some, pl.ds(0, two), :, pl.ds(0, columns)].reshape(-1, columns) for which in (0, 1))
            where = list(at)
            where[min(ORDERS[stream][:2])] = some
            where = tuple(where)
            for j, (rows, w) in enumerate(((x, wg_ref), (x, wu_ref), (dy, wd_ref))):
                value = dot(rows[:, :depth], w[:, part], ((1,), (1,))).reshape(step, two, 16, units)
                acc[(j,) + where] = acc[(j,) + where] + value
            if columns > depth:
                lane = lax.broadcasted_iota(jnp.int32, (step * two * 16, LANES), 1)
                picked = jnp.where(lane == expert, x[:, depth:].astype(jnp.float32), 0.0)
                c_ref[where] = jnp.sum(picked, axis=1, keepdims=True).reshape(step, two, 16, 1)

    for message in plan.first:
        ring(message, False).start()
    acc[...] = jnp.zeros_like(acc)
    for copy in weights + halves:
        copy.wait()
    lent = [pltpu.make_async_remote_copy(
        src_ref=ref.at[:, other_half], dst_ref=wcat.at[pl.ds((2 + i) * units, units)], send_sem=wsend.at[i], recv_sem=wrecv.at[i],
        device_id=sibling, device_id_type=MESH) for i, ref in enumerate((wg_ref, wu_ref))]
    for copy in lent:
        copy.start()
    left = {s: sum(1 for m in plan.arrived if m[0] == s and m[1] < 2) for s in range(3)}
    queue, loaded = list(tasks), []
    for message in plan.arrived:
        ring(message, True).wait_recv()
        for later in plan.after[message]:
            ring(later, False).start()
        stream, phase, piece, d, hop = message
        if phase < 2:
            left[stream] -= 1
            if left[stream] == 0:
                across((stream, None, 0), False).start()
        else:
            across((stream, piece, plan.offset(message)), False).start()
        if loaded:
            compute(loaded.pop())
        if queue and due[queue[0]] + lag < plan.time[message]:
            loaded.append(queue.pop(0))
            load(loaded[0])
    for task in queue:
        load(task)
        for before in loaded:
            compute(before)
        loaded = [task]
    compute(loaded[0])

    rows = 2 * dims[2] * 16

    def activate(x, y, store):
        part = lambda ref: ref[x, pl.ds(y, 2)].reshape(rows, ref.shape[-1])
        c = part(c_ref)
        gate_pre, up_pre, d_hidden = (part(acc.at[j]) for j in range(3))
        d_hidden = c * d_hidden
        sigma = jax.nn.sigmoid(gate_pre)
        active = gate_pre * sigma
        hidden = c * (active * up_pre)
        d_up = d_hidden * active
        d_gate = d_hidden * up_pre * sigma * (1.0 + gate_pre * (1.0 - sigma))
        if store is not None:
            for j, value in enumerate((d_gate, d_up)):
                dcat[store, pl.ds(y, 2), :, :, j * units:(j + 1) * units] = value.astype(jnp.bfloat16).reshape(2, dims[2], 16, units)
        at = pl.ds(pl.multiple_of((x * dims[1] + y) * dims[2] * 16, rows), rows)
        for j, value in enumerate((d_gate, d_up, hidden)):
            turned[j * units:(j + 1) * units, at] = value.T.astype(jnp.bfloat16)

    def swap(i):
        return pltpu.make_async_remote_copy(
            src_ref=dcat.at[i, :, :, :, pl.ds(0, 2 * units)], dst_ref=dcat.at[i, :, :, :, pl.ds(2 * units, 2 * units)],
            send_sem=dsend.at[i], recv_sem=drecv.at[i], device_id=sibling, device_id_type=MESH)

    for i in (0, 1):
        @pl.loop(0, dims[1] // 2)
        def _(pair_of):
            activate(2 * i + rep, 2 * pair_of, i)
        swap(i).start()

    spot = (place[0] // 2, place[1], place[2])
    back_starts = (0, back.tiles[0] * LANES)
    sizes = back.dims

    def moved(axis, offset):
        return lax.rem(spot[axis] + offset + sizes[axis], sizes[axis])

    def lanes(stream):
        return pl.ds(back_starts[stream], back.tiles[stream] * LANES)

    def region(stream, phase, piece, offset):
        a, b, c = BACK[stream]
        at = [None] * 3
        if phase == 0:
            at[a], at[b], at[c] = moved(a, offset), spot[b], spot[c]
        elif phase == 1:
            at[a], at[b], at[c] = moved(a, piece), moved(b, offset), spot[c]
        else:
            at[a], at[b], at[c] = slice(None), moved(b, piece), moved(c, offset)
        return tuple(at) + (slice(None), lanes(stream))

    rank = {message: i for i, message in enumerate(back.arrived)}

    def landing(message):
        stream, phase = message[:2]
        ref = land.at[rank[message]]
        columns = pl.ds(0, back.tiles[stream] * LANES)
        return ref.at[:, :, columns] if phase == 2 else ref.at[0, :, columns]

    def hand(message):
        stream, phase, piece, d, hop = message
        i = rank[message]
        axis = BACK[stream][phase]
        return pltpu.make_async_remote_copy(
            src_ref=own.at[region(stream, phase, piece, -d * hop)], dst_ref=landing(message), send_sem=bsend.at[i], recv_sem=brecv.at[i],
            device_id=neighbour(axis, -2 * d if axis == 0 else -d), device_id_type=MESH)

    made = set()

    def make(stream, offset):
        if (stream, offset) in made:
            return
        made.add((stream, offset))
        c = BACK[stream][2]
        at = (slice(None), slice(None), moved(c, offset)) if c == 2 else (slice(None), moved(c, offset))
        part = dcat[at]
        columns = back.tiles[stream] * LANES
        value = dot(part.reshape(-1, 4 * units), wcat[:, lanes(stream)], ((1,), (0,)))
        own[at + (Ellipsis, lanes(stream))] = value.astype(jnp.bfloat16).reshape(part.shape[:-1] + (columns,))

    def source(message):
        return message[0], (back.offset(message) if message[1] == 2 else 0)

    def target(message):
        stream, phase, piece, d, hop = message
        return stream, (-d * (hop - 1) if phase == 2 else 0)

    width_of = tiles_ref.shape[-1]
    count = width // width_of
    total = turned.shape[1]

    def tile(i):
        cols = pl.ds(i * width_of, width_of)
        return [pltpu.make_async_copy(g_ref.at[which, :, :, :, :, cols], tiles_ref.at[i % 2, which], tile_sem.at[i % 2, which]) for which in (0, 1)]

    def result(i):
        cols = pl.ds(i * width_of, width_of)
        return [pltpu.make_async_copy(grads_ref.at[i % 2, pl.ds(j * units, units)], ref.at[:, cols], grad_sem.at[i % 2, j])
                for j, ref in enumerate((gate_hbm, up_hbm, down_hbm))]

    def weigh(i):
        if i + 1 < count:
            for copy in tile(i + 1):
                copy.start()
        for copy in tile(i):
            copy.wait()
        if i >= 2:
            for copy in result(i - 2):
                copy.wait()
        x, dy = (tiles_ref[i % 2, which].reshape(total, width_of) for which in (0, 1))
        grads_ref[i % 2, :2 * units] = dot(turned[:2 * units], x, ((1,), (0,))).astype(jnp.bfloat16)
        grads_ref[i % 2, 2 * units:] = dot(turned[2 * units:], dy, ((1,), (0,))).astype(jnp.bfloat16)
        for copy in result(i):
            copy.start()

    for copy in tile(0):
        copy.start()
    for copy in lent:
        copy.wait()
    for i in (0, 1):
        swap(i).wait_recv()
    for message in back.first:
        make(*source(message))
        hand(message).start()
    fill = [functools.partial(activate, 2 * i + 1 - rep, y, None) for i in (0, 1) for y in range(0, dims[1], 2)]
    fill += [functools.partial(weigh, i) for i in range(count)]
    fills, filled = len(fill), 0
    rest = [(s, o) for s, _ in enumerate(BACK) for o in offsets(sizes[BACK[s][2]])]
    for number_of, message in enumerate(back.arrived):
        make(*target(message))
        for later in back.after[message]:
            make(*source(later))
        while filled < fills and filled * (len(back.arrived) - 6) < fills * number_of:
            fill[filled]()
            filled += 1
        hand(message).wait_recv()
        stream, phase, piece, d, hop = message
        at = region(stream, phase, piece, -d * (hop - 1))
        own[at] = own[at] + landing(message)[...]
        for later in back.after[message]:
            hand(later).start()

    end = pltpu.make_async_remote_copy(
        src_ref=own.at[spot], dst_ref=last, send_sem=end_send, recv_sem=end_recv, device_id=sibling, device_id_type=MESH)
    end.start()
    while filled < fills:
        fill[filled]()
        filled += 1
    for copy in copies:
        across(copy, False).wait_send()
    for message in plan.arrived:
        ring(message, False).wait_send()
    for message in back.arrived:
        hand(message).wait_send()
    for i in (0, 1):
        swap(i).wait_send()
    end.wait()
    mine = own[spot].astype(jnp.float32)
    other = last[...].astype(jnp.float32)
    rows = mine.shape[0] // 2
    left_half = jnp.where(core == 0, mine[:rows], other[rows:])
    right_half = jnp.where(core == 0, other[:rows], mine[rows:])
    each = out_ref.shape[1]
    for m in range(micro):
        out_ref[m, :, :half] = left_half[m * each:(m + 1) * each].astype(jnp.bfloat16)
        out_ref[m, :, half:] = right_half[m * each:(m + 1) * each].astype(jnp.bfloat16)
    for i in range(max(0, count - 2), count):
        for copy in result(i):
            copy.wait()


def layer(dims, tokens, grad_out, ids, gates, wg, wu, wd):
    units, width = wg.shape
    columns = width + LANES
    half = width // 2
    n = columns // LANES
    tiles = (n // 3, n // 3, n - 2 * (n // 3))
    plan = Plan(dims, ORDERS, tiles)
    narrow = half // LANES * 7 // 16
    back = Back((2,) + dims[1:], BACK, (narrow, half // LANES - narrow))
    count, back_count = len(plan.arrived), len(back.arrived)
    local = 2 * tokens.shape[0] * tokens.shape[1]
    total = dims[0] * dims[1] * dims[2] * 16
    tile = min(256, width)
    bf16 = lambda *shape: pltpu.VMEM(shape, jnp.bfloat16)
    like = lambda a: pltpu.VMEM(a.shape, a.dtype)
    sems = lambda *n: pltpu.SemaphoreType.DMA(n)
    one = pltpu.SemaphoreType.DMA
    vmem, hbm = pl.BlockSpec(memory_space=pltpu.VMEM), pl.BlockSpec(memory_space=pl.ANY)
    grad = jax.ShapeDtypeStruct((units, width), jnp.bfloat16)
    return pl.pallas_call(
        functools.partial(layer_kernel, dims, plan, back, 4.0),
        out_shape=(
            jax.ShapeDtypeStruct((2,) + dims + (16, columns), jnp.bfloat16),
            jax.ShapeDtypeStruct(tokens.shape, jnp.bfloat16),
            grad, grad, grad,
        ),
        in_specs=[hbm] * 7,
        out_specs=(hbm, vmem, hbm, hbm, hbm),
        scratch_shapes=[
            like(tokens), like(grad_out), like(ids), like(gates),
            bf16(local, columns), bf16(local, columns), bf16(local, columns),
            bf16(units, width), bf16(units, width), bf16(units, width),
            bf16(4 * units, half),
            bf16(2, 2, max(dims[0], dims[1]), max(dims[1], dims[2]), 16, max(tiles) * LANES),
            pltpu.VMEM((3,) + dims + (16, units), jnp.float32),
            pltpu.VMEM(dims + (16, 1), jnp.float32),
            bf16(2, dims[1], dims[2], 16, 4 * units),
            bf16(3 * units, total),
            bf16(2, 2, *dims, 16, tile),
            bf16(2, 3 * units, tile),
            bf16(2, dims[1], dims[2], 16, half),
            bf16(back_count, 2, 16, max(back.tiles) * LANES),
            bf16(16, half),
            sems(4), sems(3), sems(2), sems(2), sems(2), one, one, one,
            sems(count), sems(count), sems(count), sems(count), sems(2, 2),
            sems(2), sems(2), sems(back_count), sems(back_count), sems(2, 2), sems(2, 3), one, one,
        ],
        compiler_params=pltpu.CompilerParams(collective_id=0, has_side_effects=True, vmem_limit_bytes=60 << 20),
    )(tokens, grad_out, ids, gates, wg, wu, wd)


def body(tokens, grad_out, expert_ids, gate_weights, w_gate, w_up, w_down):
    dims = (2 * lax.axis_size("rep"), lax.axis_size("seq") // 2, lax.axis_size("expert") // 2)
    _, d_tokens, *grads = layer(dims, tokens, grad_out, expert_ids, gate_weights, w_gate[0], w_up[0], w_down[0])
    return (d_tokens,) + tuple(g[None] for g in grads)


def solution(mesh):
    rows = P(None, ALL, None)
    weights = P("expert", "seq", None)
    return jax.shard_map(
        body,
        mesh=mesh,
        in_specs=(rows, rows, rows, rows, weights, weights, weights),
        out_specs=(rows, weights, weights, weights),
        check_vma=False,
    )
```

```python
import functools
import heapq
import itertools

import jax
import jax.numpy as jnp
from jax import lax
from jax.experimental import pallas as pl
from jax.experimental.pallas import tpu as pltpu
from jax.sharding import PartitionSpec as P

MESH = pl.DeviceIdType.MESH
LANES = 128
ALL = ("seq", "expert", "rep")

ORDERS = ((0, 1, 2), (0, 2, 1), (0, 2, 1))
BACK = ((0, 1, 2), (0, 2, 1))


def offsets(n):
    return [0] + [d * k for k in range(1, n // 2) for d in (1, -1)] + [n // 2]


def reaches(n, turn):
    return [(d, m) for d, m in ((1, n // 2 - turn % 2), (-1, n // 2 - 1 + turn % 2)) if m]


class Plan:
    def __init__(self, dims, orders, tiles, starts=(0.0, 0.0, 0.0), unit=0.0862, latency=1.75):
        self.dims, self.orders, self.tiles, self.unit, self.latency = dims, orders, tiles, unit, latency
        self.arrived, self.after, self.time, self.whole = [], {}, {}, {}
        link, ready, pending, got, tick = {}, [], [], {}, itertools.count()

        def begin(now, stream, phase, piece):
            first = [(stream, phase, piece, d, 1) for d, _ in self.ways(stream, phase, piece)]
            for message in first:
                heapq.heappush(ready, (now, next(tick), message))
            return first

        self.first = [m for s in range(len(orders)) for phase in (0, 1) for m in begin(starts[s], s, phase, 0)]
        while ready or pending:
            if ready and (not pending or ready[0][0] <= pending[0][0]):
                now, _, message = heapq.heappop(ready)
                heapq.heappush(pending, (self.sent(link, now, message), next(tick), message))
                continue
            now, _, message = heapq.heappop(pending)
            self.arrived.append(message)
            self.time[message] = now
            stream, phase, piece, d, hop = message
            sets_off, whole = [], []
            if hop < dict(self.ways(stream, phase, piece))[d]:
                sets_off.append((stream, phase, piece, d, hop + 1))
                heapq.heappush(ready, (now, next(tick), sets_off[0]))
            off = self.offset(message)
            got[stream, phase, off] = got.get((stream, phase, off), 0) + 1
            got[stream, phase] = got.get((stream, phase), 0) + 1
            if phase == 0:
                sets_off += begin(now, stream, 1, off)
                if got[stream, 0] == self.ring(stream, 0) - 1:
                    sets_off += begin(now, stream, 2, 0)
                    whole.append((stream, 0, 0))
            elif phase == 1 and got[stream, 1, off] == self.ring(stream, 0):
                sets_off += begin(now, stream, 2, off)
                whole.append((stream, off, 0))
            elif phase == 2:
                whole.append((stream, piece, off))
            self.after[message], self.whole[message] = sets_off, whole

    def ring(self, stream, phase):
        return self.dims[self.orders[stream][phase]]

    def ways(self, stream, phase, piece):
        turn = offsets(self.ring(stream, phase - 1)).index(piece) if phase else 0
        return reaches(self.ring(stream, phase), turn)

    def sent(self, link, now, message):
        stream, phase, _, d, _ = message
        key = self.orders[stream][phase], d
        link[key] = max(now, link.get(key, 0.0)) + self.unit * self.tiles[stream] * (self.ring(stream, 0) if phase == 2 else 1)
        return link[key] + self.latency

    def offset(self, message):
        stream, phase, _, d, hop = message
        n = self.ring(stream, phase)
        return n // 2 if 2 * hop == n else -d * hop


class Back(Plan):
    def __init__(self, *args):
        super().__init__(*args)
        messages = list(reversed(self.arrived))
        self.needs = {m: self.needed(m) for m in messages}
        self.first = [m for m in messages if not self.needs[m]]
        link, done, came = {}, set(), []
        ready = [(0.0, i, m) for i, m in enumerate(messages) if not self.needs[m]]
        rank = {m: i for i, m in enumerate(messages)}
        pending, started = [], set(self.first)
        while ready or pending:
            if ready and (not pending or ready[0][0] <= pending[0][0]):
                now, i, message = heapq.heappop(ready)
                heapq.heappush(pending, (self.sent(link, now, message), i, message))
                continue
            now, _, message = heapq.heappop(pending)
            done.add(message)
            came.append(message)
            self.time[message] = now
            self.after[message] = [m for m in messages if m not in started and self.needs[m] <= done]
            for m in self.after[message]:
                started.add(m)
                heapq.heappush(ready, (now, rank[m], m))
        self.arrived = came

    def needed(self, message):
        stream, phase, piece, d, hop = message
        off = self.offset(message)
        needs = set()
        if hop < dict(self.ways(stream, phase, piece))[d]:
            needs.add((stream, phase, piece, d, hop + 1))
        if phase < 2:
            needs |= {(stream, phase + 1, off, way, 1) for way, _ in self.ways(stream, phase + 1, off)}
        if phase == 0:
            needs |= {(stream, 2, 0, way, 1) for way, _ in self.ways(stream, 2, 0)}
        return needs


def dot(a, b, dims):
    return lax.dot_general(a, b, (dims, ((), ())), preferred_element_type=jnp.float32)


def layer_kernel(dims, plan, back, kept,
                 tok_hbm, grad_hbm, ids_hbm, gates_hbm, wg_hbm, wu_hbm, wd_hbm,
                 g_ref, out_ref, gate_hbm, up_hbm, down_hbm,
                 tok_ref, grad_ref, ids_ref, gates_ref, block, got, both, wg_ref, wu_ref, wd_ref, wcat, stage, acc, c_ref,
                 dcat, turned, tiles_ref, grads_ref, sums, own, land, last,
                 in_sem, weight_sem, half_sem, wsend, wrecv, pair_send, pair_recv, local,
                 send, recv, sib_send, sib_recv, xsend, xrecv, first_send, first_recv, load_sem, dsend, drecv, bsend, brecv, tile_sem, grad_sem, end_send, end_recv):
    units, width = wg_ref.shape
    half = width // 2
    micro = tok_ref.shape[0]
    tiles = plan.tiles
    starts = [0, tiles[0] * LANES, (tiles[0] + kept) * LANES]
    seq, expert, rep = lax.axis_index("seq"), lax.axis_index("expert"), lax.axis_index("rep")
    core = lax.rem(seq, 2)
    place = (2 * (expert // dims[2]) + rep, seq // 2, lax.rem(expert, dims[2]))

    def many(pairs, sem):
        return [pltpu.make_async_copy(a, b, sem.at[i]) for i, (a, b) in enumerate(pairs)]

    inputs = many(((tok_hbm, tok_ref), (grad_hbm, grad_ref), (ids_hbm, ids_ref), (gates_hbm, gates_ref)), in_sem)
    weights = many(((wg_hbm, wg_ref), (wu_hbm, wu_ref), (wd_hbm, wd_ref)), weight_sem)
    mine_half = pl.ds(pl.multiple_of(core * half, LANES), half)
    other_half = pl.ds(pl.multiple_of((1 - core) * half, LANES), half)
    halves = many(((wg_hbm.at[:, mine_half], wcat.at[pl.ds(0, units)]), (wu_hbm.at[:, mine_half], wcat.at[pl.ds(units, units)])), half_sem)
    for copy in inputs:
        copy.start()

    def device(at, which):
        x, y, z = at
        return {"seq": 2 * y + which, "expert": (x // 2) * dims[2] + z, "rep": lax.rem(x, 2)}

    def shifted(axis, offset):
        return lax.rem(place[axis] + offset + dims[axis], dims[axis])

    def neighbour(axis, d):
        at = list(place)
        at[axis] = shifted(axis, d)
        return device(at, core)

    sibling = device(place, 1 - core)
    around = [sibling] + [neighbour(axis, d) for axis in range(3) for d in (1, -1)] + [neighbour(0, 2)]
    barrier = pltpu.get_barrier_semaphore()
    for other in around:
        pl.semaphore_signal(barrier, inc=1, device_id=other, device_id_type=MESH)
    for copy in inputs:
        copy.wait()

    rows_of = lambda ref: jnp.concatenate([ref[m].astype(jnp.float32) for m in range(micro)], axis=0)
    ids = jnp.concatenate([ids_ref[m] for m in range(micro)], axis=0)
    gates = rows_of(gates_ref)
    lane = lax.broadcasted_iota(jnp.int32, (ids.shape[0], LANES), 1)
    coeff = jnp.zeros(lane.shape, jnp.float32)
    for k in range(ids.shape[1]):
        coeff = coeff + jnp.where(lane == ids[:, k:k + 1], gates[:, k:k + 1], 0.0)
    block[:, :width] = jnp.concatenate([rows_of(tok_ref), rows_of(grad_ref)], axis=0).astype(jnp.bfloat16)
    block[:, width:] = jnp.concatenate([coeff, jnp.zeros_like(coeff)], axis=0).astype(jnp.bfloat16)
    pl.semaphore_wait(barrier, len(around))

    pair = pltpu.make_async_remote_copy(
        src_ref=block, dst_ref=got, send_sem=pair_send, recv_sem=pair_recv, device_id=sibling, device_id_type=MESH)
    pair.start()
    for copy in weights + halves:
        copy.start()
    pair.wait()
    mine, other = block[...].astype(jnp.float32), got[...].astype(jnp.float32)
    first = jnp.where(core == 0, mine, other)
    second = jnp.where(core == 0, other, mine)
    rows = block.shape[0] // 2
    upper = jnp.concatenate([first[:rows], second[:rows]], axis=0)
    lower = jnp.concatenate([first[rows:], second[rows:]], axis=0)
    both[...] = jnp.where(core == 0, upper, lower).astype(jnp.bfloat16)
    spot = (place[0] // 2, place[1], place[2])
    sizes = (2,) + dims[1:]
    west = lax.rem(spot[0] + 1 + rep, 2)
    copy = pltpu.make_async_copy(both, g_ref.at[(core, 0) + spot], local)
    copy.start()
    copy.wait()

    def moved(axis, offset, base=None):
        return lax.rem((spot[axis] if base is None else base) + offset + sizes[axis], sizes[axis])

    def turn(axis, d):
        return neighbour(axis, 2 if axis == 0 else d)

    def lanes_of(stream, crossing=False):
        return pl.ds(starts[stream], (kept if crossing and stream == 1 else tiles[stream]) * LANES)

    def chunk(stream, phase, piece, offset):
        a, b, c = ORDERS[stream]
        at = [None] * 3
        base = west if stream == 2 else None
        if phase == 0:
            at[a], at[b], at[c] = moved(a, offset, base), spot[b], spot[c]
        elif phase == 1:
            at[a], at[b], at[c] = moved(a, piece, base), moved(b, offset), spot[c]
        else:
            at[a], at[b], at[c] = slice(None), slice(None) if piece is None else moved(b, piece), moved(c, offset)
        return tuple(at)

    def place_in(which, group, stream, at, crossing=False):
        return g_ref.at[(which, group) + at + (slice(None), lanes_of(stream, crossing))]

    number = {message: i for i, message in enumerate(plan.arrived)}

    def ring(message, incoming):
        stream, phase, piece, d, hop = message
        if stream == 2 and phase == 0:
            target = place_in(core, 1, 2, chunk(2, 0, 0, -1) if incoming else spot)
            i = number[message]
            return pltpu.make_async_remote_copy(
                src_ref=place_in(core, 0, 2, spot), dst_ref=target, send_sem=send.at[i], recv_sem=recv.at[i],
                device_id=neighbour(0, -1), device_id_type=MESH)
        ref = place_in(core, stream // 2, stream, chunk(stream, phase, piece, -d * (hop if incoming else hop - 1)))
        i = number[message]
        return pltpu.make_async_remote_copy(
            src_ref=ref, dst_ref=ref, send_sem=send.at[i], recv_sem=recv.at[i],
            device_id=turn(ORDERS[stream][phase], d), device_id_type=MESH)

    units_in = sorted(((plan.time[m], u) for m in plan.arrived for u in plan.whole[m]), key=lambda pair: pair[0])
    crossing = [u for _, u in units_in if u[0] < 2]
    ready_at = {u: t for t, u in units_in}
    side = {u: 1 if i % 2 == 0 else -1 for i, u in enumerate(crossing)}
    order_of = {u: i for i, u in enumerate(crossing)}
    cross_time, busy = {}, {1: 0.0, -1: 0.0}
    for u in crossing:
        size = 2 * (kept if u[0] == 1 else tiles[u[0]]) * plan.unit
        busy[side[u]] = max(busy[side[u]], ready_at[u]) + size
        cross_time[u] = busy[side[u]] + plan.latency

    def cross(u):
        stream, piece, offset = u
        at = chunk(stream, 2, piece, offset)
        i = order_of[u]
        return pltpu.make_async_remote_copy(
            src_ref=place_in(core, 0, stream, at, True), dst_ref=place_in(core, 1, stream, at, True),
            send_sem=xsend.at[i], recv_sem=xrecv.at[i], device_id=neighbour(0, side[u]), device_id_type=MESH)

    copies = [(0, u) for u in crossing] + [(1, u) for u in crossing] + [(1, u) for _, u in units_in if u[0] == 2]
    place_of = {copy: i for i, copy in enumerate(copies)}

    def across(copy, incoming):
        group, (stream, piece, offset) = copy
        ref = place_in(1 - core if incoming else core, group, stream, chunk(stream, 2, piece, offset), group == 1)
        i = place_of[copy]
        return pltpu.make_async_remote_copy(
            src_ref=ref, dst_ref=ref, send_sem=sib_send.at[i], recv_sem=sib_recv.at[i],
            device_id=sibling, device_id_type=MESH)

    due = {}
    for group, u in copies:
        key = group, u[0], u[2]
        due[key] = max(due.get(key, 0.0), ready_at[u] if group == 0 or u[0] == 2 else cross_time[u])
    tasks = sorted(due, key=lambda key: due[key])

    def shape_of(stream):
        return 2, dims[ORDERS[stream][1]]

    def fetch(task):
        group, stream, offset = task
        slot = tasks.index(task) % 2
        one, two = shape_of(stream)
        return [pltpu.make_async_copy(
            place_in(which, group, stream, chunk(stream, 2, None, offset), group == 1),
            stage.at[slot, which, :, pl.ds(0, two), :, pl.ds(0, lanes_of(stream, group == 1).size)],
            load_sem.at[slot, which]) for which in (0, 1)]

    def load(task):
        for copy in copies:
            if (copy[0], copy[1][0], copy[1][2]) == task:
                across(copy, True).wait_recv()
        for copy in fetch(task):
            copy.start()

    def compute(task):
        group, stream, offset = task
        slot = tasks.index(task) % 2
        one, two = shape_of(stream)
        for copy in fetch(task):
            copy.wait()
        where = chunk(stream, 2, None, offset)
        columns = lanes_of(stream, group == 1).size
        depth = min(columns, width - starts[stream])
        part = pl.ds(starts[stream], depth)
        x, dy = (stage[slot, which, :, pl.ds(0, two), :, pl.ds(0, columns)].reshape(-1, columns) for which in (0, 1))
        for j, (rows, w) in enumerate(((x, wg_ref), (x, wu_ref), (dy, wd_ref))):
            value = dot(rows[:, :depth], w[:, part], ((1,), (1,))).reshape(one, two, 16, units)
            acc[(j, group) + where] = acc[(j, group) + where] + value
        if columns > depth:
            lane = lax.broadcasted_iota(jnp.int32, (one * two * 16, LANES), 1)
            picked = jnp.where(lane == expert, x[:, depth:].astype(jnp.float32), 0.0)
            c_ref[(group,) + where] = jnp.sum(picked, axis=1, keepdims=True).reshape(one, two, 16, 1)

    opening = pltpu.make_async_remote_copy(
        src_ref=place_in(core, 0, 2, spot), dst_ref=place_in(core, 1, 2, spot), send_sem=first_send, recv_sem=first_recv,
        device_id=neighbour(0, 1), device_id_type=MESH)
    opening_in = pltpu.make_async_remote_copy(
        src_ref=place_in(core, 0, 2, spot), dst_ref=place_in(core, 1, 2, (west,) + spot[1:]), send_sem=first_send, recv_sem=first_recv,
        device_id=neighbour(0, 1), device_id_type=MESH)

    rows = 2 * dims[2] * 16

    def activate(group, x, y):
        part = lambda ref: ref[group, x, pl.ds(y, 2)].reshape(rows, ref.shape[-1])
        c = part(c_ref)
        gate_pre, up_pre, d_hidden = (part(acc.at[j]) for j in range(3))
        d_hidden = c * d_hidden
        sigma = jax.nn.sigmoid(gate_pre)
        active = gate_pre * sigma
        hidden = c * (active * up_pre)
        d_up = d_hidden * active
        d_gate = d_hidden * up_pre * sigma * (1.0 + gate_pre * (1.0 - sigma))
        if group == 0:
            for j, value in enumerate((d_gate, d_up)):
                dcat[x, pl.ds(y, 2), :, :, j * units:(j + 1) * units] = value.astype(jnp.bfloat16).reshape(2, dims[2], 16, units)
        at = pl.ds((x * dims[1] + y) * dims[2] * 16, rows)
        for j, value in enumerate((d_gate, d_up, hidden)):
            turned[group, j * units:(j + 1) * units, at] = value.T.astype(jnp.bfloat16)

    def swap(i):
        return pltpu.make_async_remote_copy(
            src_ref=dcat.at[i, :, :, :, pl.ds(0, 2 * units)], dst_ref=dcat.at[i, :, :, :, pl.ds(2 * units, 2 * units)],
            send_sem=dsend.at[i], recv_sem=drecv.at[i], device_id=sibling, device_id_type=MESH)

    back_starts = (0, back.tiles[0] * LANES)
    def lanes(stream):
        return pl.ds(back_starts[stream], back.tiles[stream] * LANES)

    def region(stream, phase, piece, offset):
        a, b, c = BACK[stream]
        at = [None] * 3
        if phase == 0:
            at[a], at[b], at[c] = moved(a, offset), spot[b], spot[c]
        elif phase == 1:
            at[a], at[b], at[c] = moved(a, piece), moved(b, offset), spot[c]
        else:
            at[a], at[b], at[c] = slice(None), moved(b, piece), moved(c, offset)
        return tuple(at) + (slice(None), lanes(stream))

    rank = {message: i for i, message in enumerate(back.arrived)}

    def landing(message):
        stream, phase = message[:2]
        ref = land.at[rank[message]]
        columns = pl.ds(0, back.tiles[stream] * LANES)
        return ref.at[:, :, columns] if phase == 2 else ref.at[0, :, columns]

    def hand(message):
        stream, phase, piece, d, hop = message
        i = rank[message]
        axis = BACK[stream][phase]
        return pltpu.make_async_remote_copy(
            src_ref=own.at[region(stream, phase, piece, -d * hop)], dst_ref=landing(message), send_sem=bsend.at[i], recv_sem=brecv.at[i],
            device_id=turn(axis, -d), device_id_type=MESH)

    def make(i):
        swap(i).wait_recv()
        rows = dcat[i].reshape(-1, 4 * units)
        wide = min(512, half)

        @pl.loop(0, half // wide)
        def _(k):
            cols = pl.ds(pl.multiple_of(k * wide, wide), wide)
            value = dot(rows, wcat[:, cols], ((1,), (0,)))
            own[i, :, :, :, cols] = value.astype(jnp.bfloat16).reshape(dims[1], dims[2], 16, wide)

    width_of = tiles_ref.shape[-1]
    count = width // width_of

    def tile(group, i):
        cols = pl.ds(i * width_of, width_of)
        return [pltpu.make_async_copy(g_ref.at[which, group, :, :, :, :, cols], tiles_ref.at[i % 2, which], tile_sem.at[i % 2, which]) for which in (0, 1)]

    def result(i):
        cols = pl.ds(i * width_of, width_of)
        return [pltpu.make_async_copy(grads_ref.at[i % 2, pl.ds(j * units, units)], ref.at[:, cols], grad_sem.at[i % 2, j])
                for j, ref in enumerate((gate_hbm, up_hbm, down_hbm))]

    def weigh(group, i):
        if i == 0:
            for copy in tile(group, 0):
                copy.start()
        if i + 1 < count:
            for copy in tile(group, i + 1):
                copy.start()
        for copy in tile(group, i):
            copy.wait()
        if group == 1 and i >= 2:
            for copy in result(i - 2):
                copy.wait()
        x, dy = (tiles_ref[i % 2, which].reshape(-1, width_of) for which in (0, 1))
        cols = pl.ds(i * width_of, width_of)
        for low, high, rows in ((0, 2 * units, x), (2 * units, 3 * units, dy)):
            value = dot(turned[group, low:high], rows, ((1,), (0,)))
            if group == 0:
                sums[low:high, cols] = value
            else:
                grads_ref[i % 2, low:high] = (sums[low:high, cols] + value).astype(jnp.bfloat16)
        if group == 1:
            for copy in result(i):
                copy.start()

    opening.start()
    for message in plan.first:
        if message[0] < 2 or message[1] == 0:
            ring(message, False).start()
    acc[...] = jnp.zeros_like(acc)
    for copy in weights + halves:
        copy.wait()
    lent = [pltpu.make_async_remote_copy(
        src_ref=ref.at[:, other_half], dst_ref=wcat.at[pl.ds((2 + i) * units, units)], send_sem=wsend.at[i], recv_sem=wrecv.at[i],
        device_id=sibling, device_id_type=MESH) for i, ref in enumerate((wg_ref, wu_ref))]
    for copy in lent:
        copy.start()

    waiting, flying = {1: [], -1: []}, {1: 0, -1: 0}

    def cross_more(d):
        while waiting[d] and flying[d] < 99:
            cross(waiting[d].pop(0)).start()
            flying[d] += 1

    loaded = []

    def begin_task(task):
        load(task)
        finish_task()
        loaded.append(task)

    def finish_task():
        if loaded:
            compute(loaded.pop())

    def on_ring(message):
        ring(message, True).wait_recv()
        for later in plan.after[message]:
            ring(later, False).start()
        for u in plan.whole[message]:
            across((u[0] // 2, u), False).start()
            if u[0] < 2:
                waiting[side[u]].append(u)
                cross_more(side[u])

    def on_cross(u):
        cross(u).wait_recv()
        across((1, u), False).start()
        flying[side[u]] -= 1
        cross_more(side[u])

    def on_opening():
        opening_in.wait_recv()
        for message in plan.first:
            if message[0] == 2 and message[1] > 0:
                ring(message, False).start()

    def on_swap():
        for copy in lent:
            copy.wait()
        make(0)

    def on_first(message):
        hand(message).start()

    def on_back(message):
        hand(message).wait_recv()
        stream, phase, piece, d, hop = message
        at = region(stream, phase, piece, -d * (hop - 1))
        own[at] = own[at] + landing(message)[...]
        for later in back.after[message]:
            hand(later).start()

    end = pltpu.make_async_remote_copy(
        src_ref=own.at[spot], dst_ref=last, send_sem=end_send, recv_sem=end_recv, device_id=sibling, device_id_type=MESH)
    act = functools.partial
    line = [(plan.time[m], act(on_ring, m)) for m in plan.arrived]
    line += [(cross_time[u], act(on_cross, u)) for u in crossing]
    line += [(min(plan.time[m] for m in plan.arrived if m[0] == 2) - 0.01, on_opening)]
    line += [(due[task] + 4.0, act(begin_task, task)) for task in tasks]
    settled = max(due[task] for task in tasks if task[0] == 0) + 4.0
    steps = [finish_task, act(activate, 0, 0, 0), act(activate, 0, 0, 2), lambda: swap(0).start(),
             act(activate, 0, 1, 0), act(activate, 0, 1, 2), lambda: swap(1).start()]
    line += [(settled + 0.01 + 0.8 * i, step) for i, step in enumerate(steps)]
    go = settled + 9.0
    line += [(go - 2.0, on_swap), (go - 0.01, act(make, 1))]
    line += [(go + 0.1 * i, act(on_first, m)) for i, m in enumerate(back.first)]
    base = go + 0.1 * len(back.first)
    line += [(base + back.time[m], act(on_back, m)) for m in back.arrived]
    finish = base + max(back.time.values())
    line += [(finish + 0.01, end.start)]
    line += [(base + 1.0 + (finish - base) * i / count, act(weigh, 0, i)) for i in range(count)]
    for _, step in sorted(line, key=lambda pair: pair[0]):
        step()
    finish_task()
    for x in range(2):
        for y in range(0, dims[1], 2):
            activate(1, x, y)
    for i in range(count):
        weigh(1, i)

    for copy in copies:
        across(copy, False).wait_send()
    for message in plan.arrived:
        ring(message, False).wait_send()
    for u in crossing:
        cross(u).wait_send()
    opening.wait_send()
    for message in back.arrived:
        hand(message).wait_send()
    for i in (0, 1):
        swap(i).wait_send()
    end.wait()
    mine = own[spot].astype(jnp.float32)
    other = last[...].astype(jnp.float32)
    rows = mine.shape[0] // 2
    left_half = jnp.where(core == 0, mine[:rows], other[rows:])
    right_half = jnp.where(core == 0, other[:rows], mine[rows:])
    each = out_ref.shape[1]
    for m in range(micro):
        out_ref[m, :, :half] = left_half[m * each:(m + 1) * each].astype(jnp.bfloat16)
        out_ref[m, :, half:] = right_half[m * each:(m + 1) * each].astype(jnp.bfloat16)
    for i in range(max(0, count - 2), count):
        for copy in result(i):
            copy.wait()


def layer(dims, tokens, grad_out, ids, gates, wg, wu, wd):
    units, width = wg.shape
    columns = width + LANES
    half = width // 2
    n = columns // LANES
    late = max(2, n * 5 // 33)
    first = n * 14 // 33
    kept = n - first - late
    grid = (2,) + dims[1:]
    quiet = max(Plan(grid, ORDERS[:2], (first, n - first)).time.values()) - 6.0
    plan = Plan(grid, ORDERS, (first, n - first, late), (0.0, 0.0, quiet))
    narrow = half // LANES * 7 // 16
    back = Back(grid, BACK, (narrow, half // LANES - narrow))
    count, back_count = len(plan.arrived), len(back.arrived)
    units_in = [u for m in plan.arrived for u in plan.whole[m]]
    crossed = sum(1 for u in units_in if u[0] < 2)
    passed = len(units_in) + crossed
    local = 2 * tokens.shape[0] * tokens.shape[1]
    total = dims[0] * dims[1] * dims[2] * 16
    tile = min(512, width)
    bf16 = lambda *shape: pltpu.VMEM(shape, jnp.bfloat16)
    like = lambda a: pltpu.VMEM(a.shape, a.dtype)
    sems = lambda *n: pltpu.SemaphoreType.DMA(n)
    one = pltpu.SemaphoreType.DMA
    vmem, hbm = pl.BlockSpec(memory_space=pltpu.VMEM), pl.BlockSpec(memory_space=pl.ANY)
    grad = jax.ShapeDtypeStruct((units, width), jnp.bfloat16)
    return pl.pallas_call(
        functools.partial(layer_kernel, dims, plan, back, kept),
        out_shape=(
            jax.ShapeDtypeStruct((2, 2) + grid + (16, columns), jnp.bfloat16),
            jax.ShapeDtypeStruct(tokens.shape, jnp.bfloat16),
            grad, grad, grad,
        ),
        in_specs=[hbm] * 7,
        out_specs=(hbm, vmem, hbm, hbm, hbm),
        scratch_shapes=[
            like(tokens), like(grad_out), like(ids), like(gates),
            bf16(local, columns), bf16(local, columns), bf16(local, columns),
            bf16(units, width), bf16(units, width), bf16(units, width),
            bf16(4 * units, half),
            bf16(2, 2, 2, max(dims[1:]), 16, max(plan.tiles) * LANES),
            pltpu.VMEM((3, 2) + grid + (16, units), jnp.float32),
            pltpu.VMEM((2,) + grid + (16, 1), jnp.float32),
            bf16(2, dims[1], dims[2], 16, 4 * units),
            bf16(2, 3 * units, total // 2),
            bf16(2, 2, *grid, 16, tile),
            bf16(2, 3 * units, tile),
            pltpu.VMEM((3 * units, width), jnp.float32),
            bf16(2, dims[1], dims[2], 16, half),
            bf16(back_count, 2, 16, max(back.tiles) * LANES),
            bf16(16, half),
            sems(4), sems(3), sems(2), sems(2), sems(2), one, one, one,
            sems(count), sems(count), sems(passed), sems(passed), sems(crossed), sems(crossed), one, one, sems(2, 2),
            sems(2), sems(2), sems(back_count), sems(back_count), sems(2, 2), sems(2, 3), one, one,
        ],
        compiler_params=pltpu.CompilerParams(collective_id=0, has_side_effects=True, vmem_limit_bytes=60 << 20),
    )(tokens, grad_out, ids, gates, wg, wu, wd)


def body(tokens, grad_out, expert_ids, gate_weights, w_gate, w_up, w_down):
    dims = (2 * lax.axis_size("rep"), lax.axis_size("seq") // 2, lax.axis_size("expert") // 2)
    _, d_tokens, *grads = layer(dims, tokens, grad_out, expert_ids, gate_weights, w_gate[0], w_up[0], w_down[0])
    return (d_tokens,) + tuple(g[None] for g in grads)


def solution(mesh):
    rows = P(None, ALL, None)
    weights = P("expert", "seq", None)
    return jax.shard_map(
        body,
        mesh=mesh,
        in_specs=(rows, rows, rows, rows, weights, weights, weights),
        out_specs=(rows, weights, weights, weights),
        check_vma=False,
    )
```
